32 devices in a mesh: gx: 2 (over core), gy: 4 (over y, x), gz: 4 (over z).
Axes of the slice: x: 2, y: 2, z: 4, core: 2. Of those that a mesh axis runs over, the one named last changes fastest.
Arguments:
- velocity: float32 [3, 128, 64, 512], P(None, 'gx', 'gy', 'gz'), may hold values from -6 to 6
- viscosity: float32 [128, 64, 512], P('gx', 'gy', 'gz'), may hold values from 0.01 to 0.3
- point_force: float32 [3, 32768], P(None, ('gx', 'gy', 'gz')), may hold values from -300 to 300
- point_offset: float32 [3, 32768], P(None, ('gx', 'gy', 'gz')), may hold values from 0 to 1
- point_cell: int32 [32768], P(('gx', 'gy', 'gz')), may hold values from 0 to 131071, as said below
- point_tile: int32 [32768, 1], P(('gx', 'gy', 'gz')), may hold values from 0 to 31, as said below
Outputs:
- new_velocity: float32 [3, 128, 64, 512], P(None, 'gx', 'gy', 'gz')
- point_velocity: float32 [3, 32768], P(None, ('gx', 'gy', 'gz'))
The draws below stay inside these ranges and needn't reach their ends.
Inputs may be any that keep to these rules, and one draw needn't show every extreme that they name: `point_tile`: the 1024 points of one device form 8 runs of 128 points in a row; each run names one tile, the 8 tiles of a device differ, the first is the device's own tile and the others differ from it by at most one in each of the three tile coordinates. `point_cell`: the cell's flat index (i * 16 + j) * 128 + k within its tile.
All inputs are finite; a program needn't handle non-finite values.
Results may differ from the reference program's by a relative error of at most 0.0003.
Values sent between devices are 32-bit elements; how exact they have to be, the bound alone decides.
A program may use at most 64 MiB of HBM per device.

```python
import math
import jax
import jax.numpy as jnp
from jax import lax

CX = 64
CY = 16
CZ = 128
PTS_DEV = 1024
NX = 128
NY = 64
NZ = 512
POINTS = 32768
CAP = 128
SLOTS = 3456
N_GX = 2
N_GY = 4
N_GZ = 4


def draw_point_tile(key, part):
    devices = N_GX * N_GY * N_GZ
    source = jnp.arange(devices, dtype=jnp.int32)
    source_a = source // (N_GY * N_GZ)
    source_b = source // N_GZ % N_GY
    source_c = source % N_GZ
    beside_all = jnp.arange(27, dtype=jnp.int32)
    step_a = beside_all // 9 - 1
    step_b = beside_all // 3 % 3 - 1
    step_c = beside_all % 3 - 1
    target_a = source_a[:, None] + step_a[None, :]
    target_b = source_b[:, None] + step_b[None, :]
    target_c = source_c[:, None] + step_c[None, :]
    inside = (target_a >= 0) & (target_a < N_GX) & (target_b >= 0) & (target_b < N_GY) & (target_c >= 0) & (target_c < N_GZ)
    scores = jax.random.randint(jax.random.fold_in(key, 11), (devices, 27), 0, 1 << 20) * 32 + beside_all[None, :]
    scores = jnp.where(inside, scores, -1)
    scores = jnp.where(beside_all[None, :] == 13, 1 << 30, scores)
    _, chosen = lax.top_k(scores, 8)
    target_tile = (target_a * N_GY + target_b) * N_GZ + target_c
    picked = jnp.take_along_axis(target_tile, chosen, axis=1)
    run_of_point = jnp.arange(PTS_DEV, dtype=jnp.int32) // CAP
    tiles = picked[:, run_of_point]
    return tiles.reshape(POINTS, 1).astype(jnp.int32)


def draw_point_cell(key, part):
    runs = POINTS // CAP
    start_i = jax.random.randint(jax.random.fold_in(key, 21), (runs,), 0, CX)
    start_j = jax.random.randint(jax.random.fold_in(key, 22), (runs,), 0, CY)
    start_k = jax.random.randint(jax.random.fold_in(key, 23), (runs,), 0, CZ)
    start_i = start_i.at[0].set(CX - 1).at[1].set(0)
    start_j = start_j.at[0].set(CY - 1).at[1].set(0)
    start_k = start_k.at[0].set(CZ - 1).at[1].set(0)
    turn_i = jax.random.randint(jax.random.fold_in(key, 24), (runs,), -1, 2)
    turn_j = jax.random.randint(jax.random.fold_in(key, 25), (runs,), -1, 2)
    turn_k = jax.random.randint(jax.random.fold_in(key, 26), (runs,), 0, 2) * 2 - 1
    along = jnp.arange(CAP, dtype=jnp.int32)
    cell_i = jnp.clip(start_i[:, None] + turn_i[:, None] * (along * CX // (2 * CAP))[None, :], 0, CX - 1)
    cell_j = jnp.clip(start_j[:, None] + turn_j[:, None] * (along * CY // (2 * CAP))[None, :], 0, CY - 1)
    cell_k = jnp.clip(start_k[:, None] + turn_k[:, None] * (along * CZ // (2 * CAP))[None, :], 0, CZ - 1)
    codes = (cell_i * CY + cell_j) * CZ + cell_k
    return codes.reshape(POINTS).astype(jnp.int32)


def shard_levels(stream_key, shape, split, low, largest):
    loudness, own = 1.0, jax.random.fold_in(stream_key, 6)
    for dim, parts in split:
        draws = jnp.exp(jax.random.uniform(jax.random.fold_in(own, dim), (parts,), jnp.float32, low / len(split), largest / len(split)))
        loudness = loudness * jnp.repeat(draws, shape[dim] // parts).reshape([-1 if axis == dim else 1 for axis in range(len(shape))])
    return loudness


def scatter_about(key, dims, width, reach, pieces=(), kind=jnp.bfloat16):
    values = width * jax.random.normal(key, dims, jnp.float32)
    if pieces:
        values = values * shard_levels(key, dims, pieces, -0.22, 0.18)
    return jnp.clip(values, -reach, reach).astype(kind)


def setup_inputs(seed: int = 0) -> dict:
    key_of = jax.random.split(jax.random.key(seed), 7)
    velocity = scatter_about(key_of[0], (3, NX, NY, NZ), 1.0, 6.0, ((1, 2), (2, 4), (3, 4)), jnp.float32)
    viscosity = jnp.clip(jnp.exp(math.log(0.3) - 3.4011974 * jax.random.uniform(key_of[1], (NX, NY, NZ), jnp.float32) ** shard_levels(key_of[1], (NX, NY, NZ), ((0, 2), (1, 4), (2, 4)), -0.2, 0.2)), 0.01, 0.3)
    point_force = scatter_about(key_of[2], (3, POINTS), 50.0, 300.0, ((1, 32),), jnp.float32)
    point_offset = jnp.clip(1.0 * jax.random.uniform(key_of[3], (3, POINTS), jnp.float32) ** shard_levels(key_of[3], (3, POINTS), ((1, 32),), -0.2, 0.2), 0.0, 1.0)
    point_cell = draw_point_cell(jax.random.fold_in(key_of[6], 71), 0)
    point_tile = draw_point_tile(jax.random.fold_in(key_of[6], 71), 0)
    return {"velocity": velocity, "viscosity": viscosity, "point_force": point_force, "point_offset": point_offset, "point_cell": point_cell, "point_tile": point_tile}


time_step = 0.1
kernel_width = 2.0
one_third = 1.0 / 3.0
two_thirds = 2.0 / 3.0


def bucket_slots(targets):
    point_order = jnp.arange(targets.shape[0], dtype=jnp.int32)
    earlier = (targets[None, :] == targets[:, None]) & (point_order[None, :] < point_order[:, None])
    return jnp.sum(earlier.astype(jnp.int32), axis=1).astype(jnp.int32)


def axis_weights(centre, cell_count):
    middles = jnp.arange(cell_count, dtype=jnp.float32) + 0.5
    scaled = (middles[None, :] - centre[:, None]) / kernel_width
    unscaled = jnp.exp(-scaled * scaled)
    return unscaled / jnp.sum(unscaled, axis=1, keepdims=True)


def point_kernels(cell_codes, offsets, first_cells, second_cells, third_cells):
    plane_cells = second_cells * third_cells
    first_index = cell_codes // plane_cells
    second_index = (cell_codes // third_cells) % second_cells
    third_index = cell_codes % third_cells
    stream_weights = axis_weights(first_index.astype(jnp.float32) + offsets[0], first_cells)
    span_weights = axis_weights(second_index.astype(jnp.float32) + offsets[1], second_cells)
    height_weights = axis_weights(third_index.astype(jnp.float32) + offsets[2], third_cells)
    plane_weights = (span_weights[:, :, None] * height_weights[:, None, :]).reshape(cell_codes.shape[0], plane_cells)
    return stream_weights, plane_weights


def spread_tile(slot_force, slot_offset, slot_cell, first_cells, second_cells, third_cells, block_size):
    slot_count = slot_force.shape[1]

    def one_block(accumulated, block_index):
        first_row = block_index * block_size
        force_block = lax.dynamic_slice_in_dim(slot_force, first_row, block_size, 1)
        offset_block = lax.dynamic_slice_in_dim(slot_offset, first_row, block_size, 1)
        code_block = lax.dynamic_slice_in_dim(slot_cell, first_row, block_size, 0)
        stream_weights, plane_weights = point_kernels(code_block, offset_block, first_cells, second_cells, third_cells)
        weighted = force_block[:, :, None] * stream_weights[None, :, :]
        accumulated = accumulated + jnp.einsum("cqi,qm->cim", weighted, plane_weights, precision=lax.Precision.HIGHEST)
        return accumulated, None

    start_value = jnp.zeros((3, first_cells, second_cells * third_cells), jnp.float32)
    accumulated, _ = lax.scan(one_block, start_value, jnp.arange(slot_count // block_size, dtype=jnp.int32))
    return accumulated.reshape(3, first_cells, second_cells, third_cells)


def sample_tile(field, slot_offset, slot_cell, block_size):
    first_cells, second_cells, third_cells = field.shape[1], field.shape[2], field.shape[3]
    flat_field = field.reshape(3, first_cells, second_cells * third_cells)
    slot_count = slot_cell.shape[0]

    def one_block(carried, block_index):
        first_row = block_index * block_size
        offset_block = lax.dynamic_slice_in_dim(slot_offset, first_row, block_size, 1)
        code_block = lax.dynamic_slice_in_dim(slot_cell, first_row, block_size, 0)
        stream_weights, plane_weights = point_kernels(code_block, offset_block, first_cells, second_cells, third_cells)
        partial_sums = jnp.einsum("cim,qm->ciq", flat_field, plane_weights, precision=lax.Precision.HIGHEST)
        sampled = jnp.sum(partial_sums * stream_weights.T[None, :, :], axis=1)
        return carried, sampled

    _, sampled_blocks = lax.scan(one_block, None, jnp.arange(slot_count // block_size, dtype=jnp.int32))
    return sampled_blocks.transpose(1, 0, 2).reshape(3, slot_count)


def shifted(padded, dimension, distance):
    limits = [slice(None), slice(2, padded.shape[1] - 2), slice(2, padded.shape[2] - 2), slice(2, padded.shape[3] - 2)]
    limits[dimension] = slice(2 + distance, padded.shape[dimension] - 2 + distance)
    return padded[tuple(limits)]


def tendency(padded, viscosity, forcing):
    centre = shifted(padded, 1, 0)
    advection = jnp.zeros_like(centre)
    diffusion = -6.0 * centre
    for dimension in (1, 2, 3):
        ahead_one = shifted(padded, dimension, 1)
        behind_one = shifted(padded, dimension, -1)
        ahead_two = shifted(padded, dimension, 2)
        behind_two = shifted(padded, dimension, -2)
        gradient = (8.0 * (ahead_one - behind_one) - (ahead_two - behind_two)) / 12.0
        advection = advection + centre[dimension - 1][None] * gradient
        diffusion = diffusion + ahead_one + behind_one
    return viscosity[None] * diffusion - advection + forcing


def with_zeros(field):
    return jnp.pad(field, ((0, 0), (2, 2), (2, 2), (2, 2)))


def to_tiles(field):
    devices = N_GX * N_GY * N_GZ
    blocks = field.reshape(3, N_GX, CX, N_GY, CY, N_GZ, CZ).transpose(1, 3, 5, 0, 2, 4, 6)
    return blocks.reshape(devices, 3, CX, CY, CZ)


def from_tiles(tiles):
    blocks = tiles.reshape(N_GX, N_GY, N_GZ, 3, CX, CY, CZ).transpose(3, 0, 4, 1, 5, 2, 6)
    return blocks.reshape(3, NX, NY, NZ)


def tile_coordinates(tile):
    return tile // (N_GY * N_GZ), (tile // N_GZ) % N_GY, tile % N_GZ


def reference(velocity, viscosity, point_force, point_offset, point_cell, point_tile):
    devices = N_GX * N_GY * N_GZ
    targets = point_tile[:, 0].astype(jnp.int32)
    slot_rank = jax.vmap(bucket_slots)(targets.reshape(devices, PTS_DEV)).reshape(POINTS)
    source = jnp.arange(POINTS, dtype=jnp.int32) // PTS_DEV
    source_a, source_b, source_c = tile_coordinates(source)
    target_a, target_b, target_c = tile_coordinates(targets)
    neighbour = ((source_a - target_a + 1) * 3 + source_b - target_b + 1) * 3 + source_c - target_c + 1
    position = (neighbour * CAP + slot_rank).astype(jnp.int32)
    slot_force = jnp.zeros((devices, SLOTS, 3), jnp.float32).at[targets, position].set(point_force.T)
    slot_offset = jnp.zeros((devices, SLOTS, 3), jnp.float32).at[targets, position].set(point_offset.T)
    slot_force = slot_force.transpose(0, 2, 1)
    slot_offset = slot_offset.transpose(0, 2, 1)
    slot_cell = jnp.zeros((devices, SLOTS), jnp.int32).at[targets, position].set(point_cell)
    block_size = 3 * CAP
    tiles = lax.map(lambda members: spread_tile(members[0], members[1], members[2], CX, CY, CZ, block_size), (slot_force, slot_offset, slot_cell))
    forcing = from_tiles(tiles)
    section_one = velocity + time_step * tendency(with_zeros(velocity), viscosity, forcing)
    section_two = 0.75 * velocity + 0.25 * (section_one + time_step * tendency(with_zeros(section_one), viscosity, forcing))
    new_velocity = one_third * velocity + two_thirds * (section_two + time_step * tendency(with_zeros(section_two), viscosity, forcing))
    sampled = lax.map(lambda members: sample_tile(members[0], members[1], members[2], block_size), (to_tiles(new_velocity), slot_offset, slot_cell))
    point_velocity = sampled[targets, :, position].T
    return new_velocity, point_velocity
```

```python
import functools

import jax
import jax.numpy as jnp
from jax import lax
from jax.experimental import pallas as pl
from jax.experimental.pallas import tpu as pltpu
from jax.sharding import PartitionSpec as P

MESH = pl.DeviceIdType.MESH
time_step = 0.1
kernel_width = 2.0
one_third = 1.0 / 3.0
two_thirds = 2.0 / 3.0
run_count = 8


def split_by(x, n):
    if n & (n - 1) == 0:
        bits = n.bit_length() - 1
        return lax.shift_right_logical(x, jnp.int32(bits)), x & (n - 1)
    return lax.div(x, jnp.int32(n)), lax.rem(x, jnp.int32(n))


def halves(x):
    high = x.astype(jnp.bfloat16)
    low = (x - high.astype(jnp.float32)).astype(jnp.bfloat16)
    return high, low


def weights(centre, cells):
    middles = lax.broadcasted_iota(jnp.int32, (cells, centre.shape[1]), 0).astype(jnp.float32) + 0.5
    scaled = (middles - centre) / kernel_width
    unscaled = jnp.exp(-scaled * scaled)
    return unscaled / jnp.sum(unscaled, axis=0, keepdims=True)


def kernel(
    sizes,
    vel,
    visc,
    force,
    offset,
    cell,
    tile,
    out_vel,
    out_pts,
    field,
    force_acc,
    forcing,
    w_high,
    w_low,
    product,
    v_split,
    vals,
    neighbour,
    pay,
    slots,
    sampled,
    returned,
    y_send,
    y_recv,
    z_send,
    z_recv,
    z_mix,
    pay_ss,
    pay_rs,
    ret_ss,
    ret_rs,
    x_ss,
    x_rs,
    y_ss,
    y_rs,
    z_ss,
    z_rs,
):
    (na, nb, nc), (cx, cy, cz), cap = sizes
    a, b, c = (lax.axis_index(axis) for axis in ("gx", "gy", "gz"))
    where_am_i = (a, b, c)
    counts = (na, nb, nc)
    half_planes = cx // 2
    groups = half_planes // 4

    def step_of(n):
        return n // 9 - 1, n // 3 % 3 - 1, n % 3 - 1

    def inside(place):
        ok = (place[0] >= 0) & (place[0] < na)
        ok &= (place[1] >= 0) & (place[1] < nb)
        return ok & (place[2] >= 0) & (place[2] < nc)

    def target_of(n, sign):
        da, db, dc = step_of(n)
        return a + sign * da, b + sign * db, c + sign * dc

    slots[...] = jnp.zeros_like(slots)
    returned[...] = jnp.zeros_like(returned)
    y_recv[...] = jnp.zeros_like(y_recv)
    z_recv[...] = jnp.zeros_like(z_recv)
    edge = jnp.zeros((3, 2) + field.shape[3:], jnp.float32)
    for s in range(3):
        field[s, :, 0:2] = edge
        field[s, :, cx + 2 : cx + 4] = edge

    barrier = pltpu.get_barrier_semaphore()

    def greet(n, carry):
        place = target_of(n, 1)

        @pl.when(inside(place) & (n != 13))
        def _():
            pl.semaphore_signal(barrier, inc=1, device_id=place, device_id_type=MESH)

        return carry

    lax.fori_loop(0, 27, greet, 0)

    codes = cell[...]
    code_a, rest = split_by(codes, cy * cz)
    code_b, code_c = split_by(rest, cz)
    tiles = tile[...]
    tile_a, rest = split_by(tiles, nb * nc)
    tile_b, tile_c = split_by(rest, nc)
    neighbour[...] = ((tile_a - a + 1) * 3 + tile_b - b + 1) * 3 + tile_c - c + 1
    vals[...] = jnp.zeros_like(vals)
    for r in range(run_count):
        span = slice(r * cap, (r + 1) * cap)
        vals[r, 0:3, :] = force[:, span]
        for d, code in enumerate((code_a, code_b, code_c)):
            vals[r, 3 + d : 4 + d, :] = code[r : r + 1].astype(jnp.float32) + offset[d : d + 1, span]

    pl.semaphore_wait(
        barrier,
        (1 + (a > 0).astype(jnp.int32) + (a < na - 1).astype(jnp.int32))
        * (1 + (b > 0).astype(jnp.int32) + (b < nb - 1).astype(jnp.int32))
        * (1 + (c > 0).astype(jnp.int32) + (c < nc - 1).astype(jnp.int32))
        - 1,
    )

    def pay_copy(n, place):
        return pltpu.make_async_remote_copy(
            pay.at[n], slots.at[n], pay_ss.at[n], pay_rs.at[n], device_id=place, device_id_type=MESH
        )

    def send_points(n, carry):
        block = jnp.zeros(vals.shape[1:], jnp.float32)
        for r in range(run_count):
            block = jnp.where(neighbour[r : r + 1, :] == n, vals[r], block)
        pay[n] = block
        place = target_of(n, 1)

        @pl.when(inside(place) & (n != 13))
        def _():
            pay_copy(n, place).start()

        return carry

    lax.fori_loop(0, 27, send_points, 0)
    slots[13] = pay[13]

    lane = lax.broadcasted_iota(jnp.int32, (cy, cz), 1)

    def pack_plane(s, h, g, t, v):
        within = 4 * g + t
        for comp in range(3):
            y_send[s, 0, h, comp, g, 2 * t : 2 * t + 2, :] = v[comp][0:2]
            y_send[s, 1, h, comp, g, 2 * t : 2 * t + 2, :] = v[comp][cy - 2 : cy]
            moved = pltpu.roll(v[comp], 4 * within + 2, 1)
            z_send[s, h, comp] = jnp.where((lane >> 2) == within, moved, z_send[s, h, comp])

    def beside(dim, side):
        step = 2 * side - 1
        place = tuple(p + step if d == dim else p for d, p in enumerate(where_am_i))
        ok = place[dim] >= 0 if side == 0 else place[dim] < counts[dim]
        return place, ok

    def x_copy(s, side, place):
        source, target = (2, cx + 2) if side == 0 else (cx, 0)
        rows = slice(8, 8 + cy)
        return pltpu.make_async_remote_copy(
            field.at[s, :, pl.ds(source, 2), rows],
            field.at[s, :, pl.ds(target, 2), rows],
            x_ss.at[s, side],
            x_rs.at[s, side],
            device_id=place,
            device_id_type=MESH,
        )

    def y_copy(s, side, h, place):
        return pltpu.make_async_remote_copy(
            y_send.at[s, side, h],
            y_recv.at[s, side, h],
            y_ss.at[s, side, h],
            y_rs.at[s, side, h],
            device_id=place,
            device_id_type=MESH,
        )

    def z_copy(s, side, h, place):
        return pltpu.make_async_remote_copy(
            z_send.at[s, h],
            z_recv.at[s, side, h],
            z_ss.at[s, side, h],
            z_rs.at[s, side, h],
            device_id=place,
            device_id_type=MESH,
        )

    def send_half(s, h):
        for side in (0, 1):
            place, ok = beside(1, side)
            pl.when(ok)(lambda: y_copy(s, side, h, place).start())
        for side in (0, 1):
            place, ok = beside(2, side)
            pl.when(ok)(lambda: z_copy(s, side, h, place).start())
            place, ok = beside(0, side)
            pl.when(ok & (h == side))(lambda: x_copy(s, side, place).start())

    def wait_half(s, h):
        for side in (0, 1):
            place, ok = beside(0, 1 - side)
            pl.when(ok & (h == 1 - side))(lambda: x_copy(s, side, place).wait_recv())
            place, ok = beside(2, 1 - side)
            pl.when(ok)(lambda: z_copy(s, side, h, place).wait_recv())
            place, ok = beside(1, 1 - side)
            pl.when(ok)(lambda: y_copy(s, side, h, place).wait_recv())

    def wait_sends(s):
        for side in (0, 1):
            place, ok = beside(0, side)
            pl.when(ok)(lambda: x_copy(s, side, place).wait_send())
            for h in (0, 1):
                place, ok = beside(1, side)
                pl.when(ok)(lambda: y_copy(s, side, h, place).wait_send())
                place, ok = beside(2, side)
                pl.when(ok)(lambda: z_copy(s, side, h, place).wait_send())

    first = lax.rem(a, 2)
    z_send[...] = jnp.zeros_like(z_send)

    for turn in range(2):
        h = first if turn == 0 else 1 - first

        def stage_in(g, carry):
            for t in range(4):
                i = h * half_planes + 4 * g + t
                v = [vel[comp, i] for comp in range(3)]
                for comp in range(3):
                    field[0, comp, i + 2, 8 : 8 + cy, :] = v[comp]
                pack_plane(0, h, g, t, v)
            return carry

        lax.fori_loop(0, groups, stage_in, 0)
        send_half(0, h)

    def span_of(p, count):
        low = jnp.where(p < count - 1, 0, 1)
        high = jnp.where(p > 0, 2, 1)
        return low, high - low + 1

    (low_a, in_a), (low_b, in_b), (low_c, in_c) = (
        span_of(p, count) for p, count in zip(where_am_i, counts)
    )
    blocks = in_a * in_b * in_c
    pairs = (blocks + 1) // 2

    def block_of(v):
        n = (low_a + v // (in_b * in_c)) * 9 + (low_b + v // in_c % in_b) * 3 + low_c + v % in_c
        return jnp.where(v < blocks, n, 27)

    def wait_points(n, carry):
        place = target_of(n, -1)

        @pl.when(inside(place) & (n != 13))
        def _():
            pay_copy(n, place).wait_recv()

        return carry

    lax.fori_loop(0, 27, wait_points, 0)

    def pair_slots(pair):
        n0, n1 = block_of(2 * pair), block_of(2 * pair + 1)
        return n0, n1, jnp.concatenate([slots[n0], slots[n1]], axis=1)

    force_acc[...] = jnp.zeros_like(force_acc)

    def spread(pair, carry):
        _, _, s = pair_slots(pair)
        wx = weights(s[3:4], cx)
        wy = weights(s[4:5], cy)
        wz = weights(s[5:6], cz)
        a_high, a_low = halves(jnp.concatenate([s[d : d + 1] * wx for d in range(3)], axis=0))
        for j in range(cy):
            high, low = halves(wy[j : j + 1] * wz)
            w_high[j * cz : (j + 1) * cz, :] = high
            w_low[j * cz : (j + 1) * cz, :] = low
        right = jnp.concatenate([a_high, a_low, a_high], axis=1)
        left = jnp.concatenate([w_high[...], w_high[...], w_low[...]], axis=1)
        force_acc[...] += lax.dot_general(
            left, right, (((1,), (1,)), ((), ())), preferred_element_type=jnp.float32
        )
        return carry

    lax.fori_loop(0, pairs, spread, 0)

    for j in range(cy):
        turned = force_acc[j * cz : (j + 1) * cz, :].T
        for comp in range(3):
            forcing[pl.ds(comp * cx * cy + j, cx, stride=cy), :] = turned[comp * cx : (comp + 1) * cx]

    for s in range(3):
        for turn in range(2):
            h = first if turn == 0 else 1 - first
            wait_half(s, h)
            for comp in range(3):
                z_mix[comp] = jnp.where((lane & 3) < 2, z_recv[s, 1, h, comp], z_recv[s, 0, h, comp])

            def advance(g, carry):
                for t in range(4):
                    i = h * half_planes + 4 * g + t
                    centre = [field[s, comp, i + 2, 8 : 8 + cy, :] for comp in range(3)]
                    nu = visc[i]
                    result = []
                    for comp in range(3):
                        v = centre[comp]
                        field[s, comp, i + 2, 6:8, :] = y_recv[s, 1, h, comp, g, 2 * t : 2 * t + 2, :]
                        field[s, comp, i + 2, 8 + cy : 10 + cy, :] = y_recv[
                            s, 0, h, comp, g, 2 * t : 2 * t + 2, :
                        ]
                        ends = pltpu.roll(z_mix[comp], cz - 2 - 4 * (4 * g + t), 1)
                        around = (
                            [field[s, comp, i + 2 + m, 8 : 8 + cy, :] for m in (-2, -1, 1, 2)],
                            [field[s, comp, i + 2, 8 + m : 8 + m + cy, :] for m in (-2, -1, 1, 2)],
                            [
                                pltpu.roll(jnp.where(lane >= cz - 2, ends, v), 2, 1),
                                pltpu.roll(jnp.where(lane >= cz - 1, ends, v), 1, 1),
                                pltpu.roll(jnp.where(lane < 1, ends, v), cz - 1, 1),
                                pltpu.roll(jnp.where(lane < 2, ends, v), cz - 2, 1),
                            ],
                        )
                        spreading = -6.0 * v
                        carried = jnp.zeros_like(v)
                        for d in range(3):
                            m2, m1, p1, p2 = around[d]
                            carried += centre[d] * (8.0 * (p1 - m1) - (p2 - m2))
                            spreading += p1 + m1
                        row = pl.multiple_of((comp * cx + i) * cy, cy)
                        tend = nu * spreading - carried * (1.0 / 12.0) + forcing[pl.ds(row, cy), :]
                        moved = v + time_step * tend
                        if s == 1:
                            moved = 0.75 * vel[comp, i] + 0.25 * moved
                        elif s == 2:
                            moved = one_third * vel[comp, i] + two_thirds * moved
                        result.append(moved)
                        if s < 2:
                            field[s + 1, comp, i + 2, 8 : 8 + cy, :] = moved
                        else:
                            out_vel[comp, i] = moved
                            high, low = halves(moved)
                            v_split[pl.ds(row, cy), 0:cz] = high
                            v_split[pl.ds(row, cy), cz : 2 * cz] = low
                    if s < 2:
                        pack_plane(s + 1, h, g, t, result)
                return carry

            lax.fori_loop(0, groups, advance, 0)
            if s < 2:
                send_half(s + 1, h)

    def ret_copy(n, place):
        return pltpu.make_async_remote_copy(
            sampled.at[n],
            returned.at[n],
            ret_ss.at[n],
            ret_rs.at[n],
            device_id=place,
            device_id_type=MESH,
        )

    sampled[...] = jnp.zeros_like(sampled)

    def sample(pair, carry):
        n0, n1, s = pair_slots(pair)
        wx = weights(s[3:4], cx)
        wy = weights(s[4:5], cy)
        high, low = halves(weights(s[5:6], cz))
        right = jnp.concatenate([high, high, low, low], axis=0)
        for comp in range(3):
            v = v_split[comp * cx * cy : (comp + 1) * cx * cy, :]
            product[...] = jnp.dot(
                jnp.concatenate([v, v], axis=1), right, preferred_element_type=jnp.float32
            )
            total = jnp.zeros((cy, 2 * cap), jnp.float32)
            for i in range(cx):
                total += wx[i : i + 1] * product[i * cy : (i + 1) * cy, :]
            row = jnp.sum(total * wy, axis=0, keepdims=True)
            sampled[n0, comp : comp + 1, :] = row[:, :cap]
            sampled[n1, comp : comp + 1, :] = row[:, cap:]
        for n in (n0, n1):

            @pl.when((n != 13) & (n < 27))
            def _():
                ret_copy(n, target_of(n, -1)).start()

        return carry

    lax.fori_loop(0, pairs, sample, 0)
    returned[13] = sampled[13]

    def wait_returned(n, carry):
        @pl.when(inside(target_of(n, 1)) & (n != 13))
        def _():
            ret_copy(n, target_of(n, 1)).wait_recv()

        return carry

    lax.fori_loop(0, 27, wait_returned, 0)
    for r in range(run_count):

        def pick(n, block):
            return jnp.where(neighbour[r : r + 1, :] == n, returned[n], block)

        block = lax.fori_loop(0, 27, pick, jnp.zeros(returned.shape[1:], jnp.float32), unroll=True)
        out_pts[:, r * cap : (r + 1) * cap] = block[0:3]

    def finish(n, carry):
        @pl.when(inside(target_of(n, 1)) & (n != 13))
        def _():
            pay_copy(n, target_of(n, 1)).wait_send()

        @pl.when(inside(target_of(n, -1)) & (n != 13))
        def _():
            ret_copy(n, target_of(n, -1)).wait_send()

        return carry

    lax.fori_loop(0, 27, finish, 0)
    for s in range(3):
        wait_sends(s)


def per_device(velocity, viscosity, point_force, point_offset, point_cell, point_tile):
    _, cx, cy, cz = velocity.shape
    points = point_force.shape[1]
    cap = points // run_count
    mesh_sizes = tuple(lax.axis_size(axis) for axis in ("gx", "gy", "gz"))
    sizes = (mesh_sizes, (cx, cy, cz), cap)
    half, groups = cx // 2, cx // 8
    f32, bf16 = jnp.float32, jnp.bfloat16
    dma = pltpu.SemaphoreType.DMA
    whole = pl.BlockSpec(memory_space=pltpu.VMEM)
    return pl.pallas_call(
        functools.partial(kernel, sizes),
        out_shape=(
            jax.ShapeDtypeStruct(velocity.shape, f32),
            jax.ShapeDtypeStruct(point_force.shape, f32),
        ),
        in_specs=[whole] * 6,
        out_specs=(whole, whole),
        scratch_shapes=[
            pltpu.VMEM((3, 3, cx + 4, cy + 16, cz), f32),
            pltpu.VMEM((cy * cz, 3 * cx), f32),
            pltpu.VMEM((3 * cx * cy, cz), f32),
            pltpu.VMEM((cy * cz, 2 * cap), bf16),
            pltpu.VMEM((cy * cz, 2 * cap), bf16),
            pltpu.VMEM((cx * cy, 2 * cap), f32),
            pltpu.VMEM((3 * cx * cy, 2 * cz), bf16),
            pltpu.VMEM((run_count, 8, cap), f32),
            pltpu.VMEM((run_count, cap), jnp.int32),
            pltpu.VMEM((27, 8, cap), f32),
            pltpu.VMEM((28, 8, cap), f32),
            pltpu.VMEM((28, 8, cap), f32),
            pltpu.VMEM((27, 8, cap), f32),
            pltpu.VMEM((3, 2, 2, 3, groups, 8, cz), f32),
            pltpu.VMEM((3, 2, 2, 3, groups, 8, cz), f32),
            pltpu.VMEM((3, 2, 3, cy, cz), f32),
            pltpu.VMEM((3, 2, 2, 3, cy, cz), f32),
            pltpu.VMEM((3, cy, cz), f32),
            dma((27,)),
            dma((27,)),
            dma((27,)),
            dma((27,)),
            dma((3, 2)),
            dma((3, 2)),
            dma((3, 2, 2)),
            dma((3, 2, 2)),
            dma((3, 2, 2)),
            dma((3, 2, 2)),
        ],
        compiler_params=pltpu.CompilerParams(
            collective_id=0, has_side_effects=True, vmem_limit_bytes=56 * 2**20
        ),
        name="farm_step",
    )(
        velocity,
        viscosity,
        point_force,
        point_offset,
        point_cell.reshape(run_count, cap),
        point_tile.reshape(run_count, cap),
    )


def solution(mesh):
    in_specs = (
        P(None, "gx", "gy", "gz"),
        P("gx", "gy", "gz"),
        P(None, ("gx", "gy", "gz")),
        P(None, ("gx", "gy", "gz")),
        P(("gx", "gy", "gz")),
        P(("gx", "gy", "gz"), None),
    )
    out_specs = (P(None, "gx", "gy", "gz"), P(None, ("gx", "gy", "gz")))
    return jax.shard_map(
        per_device, mesh=mesh, in_specs=in_specs, out_specs=out_specs, check_vma=False
    )
```

```python
import functools

import jax
import jax.numpy as jnp
from jax import lax
from jax.experimental import pallas as pl
from jax.experimental.pallas import tpu as pltpu
from jax.sharding import PartitionSpec as P

MESH = pl.DeviceIdType.MESH
time_step = 0.1
kernel_width = 2.0
one_third = 1.0 / 3.0
two_thirds = 2.0 / 3.0
run_count = 8


def split_by(x, n):
    if n & (n - 1) == 0:
        bits = n.bit_length() - 1
        return lax.shift_right_logical(x, jnp.int32(bits)), x & (n - 1)
    return lax.div(x, jnp.int32(n)), lax.rem(x, jnp.int32(n))


def halves(x):
    high = x.astype(jnp.bfloat16)
    low = (x - high.astype(jnp.float32)).astype(jnp.bfloat16)
    return high, low


def weights(centre, cells):
    middles = lax.broadcasted_iota(jnp.int32, (cells, centre.shape[1]), 0).astype(jnp.float32) + 0.5
    scaled = (middles - centre) / kernel_width
    unscaled = jnp.exp(-scaled * scaled)
    return unscaled / jnp.sum(unscaled, axis=0, keepdims=True)


def kernel(
    sizes,
    vel,
    visc_in,
    force,
    offset,
    cell,
    tile,
    out_vel,
    out_pts,
    field,
    visc,
    fresh,
    local_sem,
    force_acc,
    forcing,
    w_high,
    w_low,
    product,
    v_split,
    vals,
    neighbour,
    pay,
    slots,
    sampled,
    returned,
    y_send,
    y_recv,
    z_send,
    z_recv,
    z_mix,
    pay_ss,
    pay_rs,
    ret_ss,
    ret_rs,
    x_ss,
    x_rs,
    y_ss,
    y_rs,
    z_ss,
    z_rs,
):
    (na, nb, nc), (cx, cy, cz), cap = sizes
    a, b, c = (lax.axis_index(axis) for axis in ("gx", "gy", "gz"))
    where_am_i = (a, b, c)
    counts = (na, nb, nc)
    rows = cy // 2
    pack_groups = cz // 16
    packs = cx // (cz // 4)

    def step_of(n):
        return n // 9 - 1, n // 3 % 3 - 1, n % 3 - 1

    def inside(place):
        ok = (place[0] >= 0) & (place[0] < na)
        ok &= (place[1] >= 0) & (place[1] < nb)
        return ok & (place[2] >= 0) & (place[2] < nc)

    def target_of(n, sign):
        da, db, dc = step_of(n)
        return a + sign * da, b + sign * db, c + sign * dc

    vel_copy = pltpu.make_async_copy(
        vel, field.at[0, :, pl.ds(2, cx), pl.ds(8, cy)], local_sem.at[0]
    )
    vel_copy.start()
    visc_copy = pltpu.make_async_copy(visc_in, visc, local_sem.at[1])
    visc_copy.start()

    slots[...] = jnp.zeros_like(slots)
    returned[...] = jnp.zeros_like(returned)
    y_recv[...] = jnp.zeros_like(y_recv)
    z_recv[...] = jnp.zeros_like(z_recv)
    edge = jnp.zeros((3, 2) + field.shape[3:], jnp.float32)
    for s in range(3):
        field[s, :, 0:2] = edge
        field[s, :, cx + 2 : cx + 4] = edge

    barrier = pltpu.get_barrier_semaphore()

    def greet(n, carry):
        place = target_of(n, 1)

        @pl.when(inside(place) & (n != 13))
        def _():
            pl.semaphore_signal(barrier, inc=1, device_id=place, device_id_type=MESH)

        return carry

    lax.fori_loop(0, 27, greet, 0)

    codes = cell[...]
    code_a, rest = split_by(codes, cy * cz)
    code_b, code_c = split_by(rest, cz)
    tiles = tile[...]
    tile_a, rest = split_by(tiles, nb * nc)
    tile_b, tile_c = split_by(rest, nc)
    neighbour[...] = ((tile_a - a + 1) * 3 + tile_b - b + 1) * 3 + tile_c - c + 1
    vals[...] = jnp.zeros_like(vals)
    for r in range(run_count):
        span = slice(r * cap, (r + 1) * cap)
        vals[r, 0:3, :] = force[:, span]
        for d, code in enumerate((code_a, code_b, code_c)):
            vals[r, 3 + d : 4 + d, :] = code[r : r + 1].astype(jnp.float32) + offset[d : d + 1, span]

    pl.semaphore_wait(
        barrier,
        (1 + (a > 0).astype(jnp.int32) + (a < na - 1).astype(jnp.int32))
        * (1 + (b > 0).astype(jnp.int32) + (b < nb - 1).astype(jnp.int32))
        * (1 + (c > 0).astype(jnp.int32) + (c < nc - 1).astype(jnp.int32))
        - 1,
    )

    def pay_copy(n, place):
        return pltpu.make_async_remote_copy(
            pay.at[n], slots.at[n], pay_ss.at[n], pay_rs.at[n], device_id=place, device_id_type=MESH
        )

    def send_points(n, carry):
        block = jnp.zeros(vals.shape[1:], jnp.float32)
        for r in range(run_count):
            block = jnp.where(neighbour[r : r + 1, :] == n, vals[r], block)
        pay[n] = block
        place = target_of(n, 1)

        @pl.when(inside(place) & (n != 13))
        def _():
            pay_copy(n, place).start()

        return carry

    lax.fori_loop(0, 27, send_points, 0)
    slots[13] = pay[13]

    lane = lax.broadcasted_iota(jnp.int32, (rows, cz), 1)

    def pack_planes(s, h, g, planes):
        inner = slice(0, 2) if h == 0 else slice(rows - 2, rows)
        pack, place = g // pack_groups, g % pack_groups
        for comp in range(3):
            packed = z_send[s, h, comp, pack]
            for t in range(4):
                v = planes[t][comp]
                y_send[s, h, comp, g, 2 * t : 2 * t + 2, :] = v[inner]
                within = 4 * place + t
                packed = jnp.where((lane >> 2) == within, pltpu.roll(v, 4 * within + 2, 1), packed)
            z_send[s, h, comp, pack] = packed

    def beside(dim, side):
        step = 2 * side - 1
        place = tuple(p + step if d == dim else p for d, p in enumerate(where_am_i))
        ok = place[dim] >= 0 if side == 0 else place[dim] < counts[dim]
        return place, ok

    def x_copy(s, side, h, place):
        source, target = (2, cx + 2) if side == 0 else (cx, 0)
        span = slice(8 + rows * h, 8 + rows * (h + 1))
        return pltpu.make_async_remote_copy(
            field.at[s, :, pl.ds(source, 2), span],
            field.at[s, :, pl.ds(target, 2), span],
            x_ss.at[s, side, h],
            x_rs.at[s, side, h],
            device_id=place,
            device_id_type=MESH,
        )

    def y_copy(s, side, place):
        return pltpu.make_async_remote_copy(
            y_send.at[s, side],
            y_recv.at[s, side],
            y_ss.at[s, side],
            y_rs.at[s, side],
            device_id=place,
            device_id_type=MESH,
        )

    def z_copy(s, side, h, place):
        return pltpu.make_async_remote_copy(
            z_send.at[s, h],
            z_recv.at[s, side, h],
            z_ss.at[s, side, h],
            z_rs.at[s, side, h],
            device_id=place,
            device_id_type=MESH,
        )

    def send_half(s, h):
        place, ok = beside(1, h)
        pl.when(ok)(lambda: y_copy(s, h, place).start())
        for side in (0, 1):
            z_place, z_ok = beside(2, side)
            pl.when(z_ok)(lambda: z_copy(s, side, h, z_place).start())
            x_place, x_ok = beside(0, side)
            pl.when(x_ok)(lambda: x_copy(s, side, h, x_place).start())

    def wait_half(s, h):
        for side in (0, 1):
            x_place, x_ok = beside(0, 1 - side)
            pl.when(x_ok)(lambda: x_copy(s, side, h, x_place).wait_recv())
            z_place, z_ok = beside(2, 1 - side)
            pl.when(z_ok)(lambda: z_copy(s, side, h, z_place).wait_recv())
        place, ok = beside(1, h)
        pl.when(ok)(lambda: y_copy(s, 1 - h, place).wait_recv())

    def wait_sends(s):
        for side in (0, 1):
            y_place, y_ok = beside(1, side)
            pl.when(y_ok)(lambda: y_copy(s, side, y_place).wait_send())
            x_place, x_ok = beside(0, side)
            z_place, z_ok = beside(2, side)
            for h in (0, 1):
                pl.when(x_ok)(lambda: x_copy(s, side, h, x_place).wait_send())
                pl.when(z_ok)(lambda: z_copy(s, side, h, z_place).wait_send())

    first = lax.rem(b, 2)

    def by_turn(turn, work):
        pl.when(first == turn)(lambda: work(0))
        pl.when(first != turn)(lambda: work(1))

    def half_of(turn):
        return first if turn == 0 else 1 - first

    z_send[...] = jnp.zeros_like(z_send)
    vel_copy.wait()

    def first_faces(h):
        def one(g, carry):
            span = slice(8 + rows * h, 8 + rows * (h + 1))
            pack_planes(
                0, h, g, [[field[0, comp, 4 * g + t + 2, span, :] for comp in range(3)] for t in range(4)]
            )
            return carry

        lax.fori_loop(0, cx // 4, one, 0)
        send_half(0, h)

    for turn in range(2):
        by_turn(turn, first_faces)

    def span_of(p, count):
        low = jnp.where(p < count - 1, 0, 1)
        high = jnp.where(p > 0, 2, 1)
        return low, high - low + 1

    (low_a, in_a), (low_b, in_b), (low_c, in_c) = (
        span_of(p, count) for p, count in zip(where_am_i, counts)
    )
    blocks = in_a * in_b * in_c
    pairs = (blocks + 1) // 2

    def block_of(v):
        n = (low_a + v // (in_b * in_c)) * 9 + (low_b + v // in_c % in_b) * 3 + low_c + v % in_c
        return jnp.where(v < blocks, n, 27)

    def wait_points(n, carry):
        place = target_of(n, -1)

        @pl.when(inside(place) & (n != 13))
        def _():
            pay_copy(n, place).wait_recv()

        return carry

    lax.fori_loop(0, 27, wait_points, 0)

    def pair_slots(pair):
        n0, n1 = block_of(2 * pair), block_of(2 * pair + 1)
        return n0, n1, jnp.concatenate([slots[n0], slots[n1]], axis=1)

    force_acc[...] = jnp.zeros_like(force_acc)
    visc_copy.wait()

    def half_rows(w, h):
        return jnp.where(h == 0, w[:rows], w[rows:])

    def spread_half(turn):
        h = half_of(turn)

        def spread(pair, carry):
            _, _, s = pair_slots(pair)
            wx = weights(s[3:4], cx)
            wy = half_rows(weights(s[4:5], cy), h)
            wz = weights(s[5:6], cz)
            a_high, a_low = halves(jnp.concatenate([s[d : d + 1] * wx for d in range(3)], axis=0))
            for j in range(rows):
                high, low = halves(wy[j : j + 1] * wz)
                w_high[j * cz : (j + 1) * cz, :] = high
                w_low[j * cz : (j + 1) * cz, :] = low
            right = jnp.concatenate([a_high, a_low, a_high], axis=1)
            left = jnp.concatenate([w_high[...], w_high[...], w_low[...]], axis=1)
            force_acc[turn] += lax.dot_general(
                left, right, (((1,), (1,)), ((), ())), preferred_element_type=jnp.float32
            )
            return carry

        lax.fori_loop(0, pairs, spread, 0)
        for j in range(rows):
            turned = force_acc[turn, j * cz : (j + 1) * cz, :].T
            for comp in range(3):
                forcing[turn, pl.ds(comp * cx * rows + j, cx, stride=rows), :] = turned[
                    comp * cx : (comp + 1) * cx
                ]

    def advance_half(s, turn, h):
        wait_half(s, h)
        for comp in range(3):
            for pack in range(packs):
                z_mix[comp, pack] = jnp.where(
                    (lane & 3) < 2, z_recv[s, 1, h, comp, pack], z_recv[s, 0, h, comp, pack]
                )
        low = 8 + rows * h
        span = slice(low, low + rows)
        halo = slice(6, 8) if h == 0 else slice(8 + cy, 10 + cy)

        def advance(g, carry):
            pack, place = g // pack_groups, g % pack_groups
            planes = []
            for t in range(4):
                i = 4 * g + t
                centre = [field[s, comp, i + 2, span, :] for comp in range(3)]
                nu = visc[i, rows * h : rows * (h + 1), :]
                result = []
                for comp in range(3):
                    v = centre[comp]
                    field[s, comp, i + 2, halo, :] = y_recv[s, 1 - h, comp, g, 2 * t : 2 * t + 2, :]
                    ends = pltpu.roll(z_mix[comp, pack], cz - 2 - 4 * (4 * place + t), 1)
                    around = (
                        [field[s, comp, i + 2 + m, span, :] for m in (-2, -1, 1, 2)],
                        [field[s, comp, i + 2, low + m : low + m + rows, :] for m in (-2, -1, 1, 2)],
                        [
                            pltpu.roll(jnp.where(lane >= cz - 2, ends, v), 2, 1),
                            pltpu.roll(jnp.where(lane >= cz - 1, ends, v), 1, 1),
                            pltpu.roll(jnp.where(lane < 1, ends, v), cz - 1, 1),
                            pltpu.roll(jnp.where(lane < 2, ends, v), cz - 2, 1),
                        ],
                    )
                    spreading = -6.0 * v
                    carried = jnp.zeros_like(v)
                    for d in range(3):
                        m2, m1, p1, p2 = around[d]
                        carried += centre[d] * (8.0 * (p1 - m1) - (p2 - m2))
                        spreading += p1 + m1
                    row = pl.multiple_of((comp * cx + i) * rows, rows)
                    tend = nu * spreading - carried * (1.0 / 12.0) + forcing[turn, pl.ds(row, rows), :]
                    moved = v + time_step * tend
                    if s == 1:
                        moved = 0.75 * field[0, comp, i + 2, span, :] + 0.25 * moved
                    elif s == 2:
                        moved = one_third * field[0, comp, i + 2, span, :] + two_thirds * moved
                    result.append(moved)
                    if s < 2:
                        field[s + 1, comp, i + 2, span, :] = moved
                    else:
                        fresh[comp, i, rows * h : rows * (h + 1), :] = moved
                planes.append(result)
            if s < 2:
                pack_planes(s + 1, h, g, planes)
            else:
                for comp in range(3):
                    for t in (0, 2):
                        row = pl.multiple_of((comp * cx + 4 * g + t) * rows, 2 * rows)
                        high, low_part = halves(
                            jnp.concatenate([planes[t][comp], planes[t + 1][comp]], axis=0)
                        )
                        v_split[turn, pl.ds(row, 2 * rows), 0:cz] = high
                        v_split[turn, pl.ds(row, 2 * rows), cz : 2 * cz] = low_part
            return carry

        lax.fori_loop(0, cx // 4, advance, 0)
        if s < 2:
            send_half(s + 1, h)
        else:
            out_copy(h).start()

    def out_copy(h):
        span = slice(rows * h, rows * (h + 1))
        return pltpu.make_async_copy(fresh.at[:, :, span], out_vel.at[:, :, span], local_sem.at[2 + h])

    def section(s, turn):
        by_turn(turn, lambda h: advance_half(s, turn, h))

    spread_half(0)
    section(0, 0)
    spread_half(1)
    section(0, 1)
    section(1, 0)
    section(1, 1)
    section(2, 0)

    def ret_copy(n, place):
        return pltpu.make_async_remote_copy(
            sampled.at[n],
            returned.at[n],
            ret_ss.at[n],
            ret_rs.at[n],
            device_id=place,
            device_id_type=MESH,
        )

    sampled[...] = jnp.zeros_like(sampled)

    def sample_half(turn):
        h = half_of(turn)

        def sample(pair, carry):
            n0, n1, s = pair_slots(pair)
            wx = weights(s[3:4], cx)
            wy = half_rows(weights(s[4:5], cy), h)
            high, low = halves(weights(s[5:6], cz))
            right = jnp.concatenate([high, high, low, low], axis=0)
            for comp in range(3):
                v = v_split[turn, comp * cx * rows : (comp + 1) * cx * rows, :]
                product[comp] = jnp.dot(
                    jnp.concatenate([v, v], axis=1), right, preferred_element_type=jnp.float32
                )
            for comp in range(3):
                total = jnp.zeros((rows, 2 * cap), jnp.float32)
                for i in range(cx):
                    total += wx[i : i + 1] * product[comp, i * rows : (i + 1) * rows, :]
                row = jnp.sum(total * wy, axis=0, keepdims=True)
                sampled[n0, comp : comp + 1, :] += row[:, :cap]
                sampled[n1, comp : comp + 1, :] += row[:, cap:]
            if turn == 1:
                for n in (n0, n1):

                    @pl.when((n != 13) & (n < 27))
                    def _():
                        ret_copy(n, target_of(n, -1)).start()

            return carry

        lax.fori_loop(0, pairs, sample, 0)

    sample_half(0)
    section(2, 1)
    sample_half(1)
    returned[13] = sampled[13]

    def wait_returned(n, carry):
        @pl.when(inside(target_of(n, 1)) & (n != 13))
        def _():
            ret_copy(n, target_of(n, 1)).wait_recv()

        return carry

    lax.fori_loop(0, 27, wait_returned, 0)
    for r in range(run_count):

        def pick(n, block):
            return jnp.where(neighbour[r : r + 1, :] == n, returned[n], block)

        block = lax.fori_loop(0, 27, pick, jnp.zeros(returned.shape[1:], jnp.float32), unroll=True)
        out_pts[:, r * cap : (r + 1) * cap] = block[0:3]

    def finish(n, carry):
        @pl.when(inside(target_of(n, 1)) & (n != 13))
        def _():
            pay_copy(n, target_of(n, 1)).wait_send()

        @pl.when(inside(target_of(n, -1)) & (n != 13))
        def _():
            ret_copy(n, target_of(n, -1)).wait_send()

        return carry

    lax.fori_loop(0, 27, finish, 0)
    for s in range(3):
        wait_sends(s)
    for h in range(2):
        out_copy(h).wait()


def per_device(velocity, viscosity, point_force, point_offset, point_cell, point_tile):
    _, cx, cy, cz = velocity.shape
    points = point_force.shape[1]
    cap = points // run_count
    mesh_sizes = tuple(lax.axis_size(axis) for axis in ("gx", "gy", "gz"))
    sizes = (mesh_sizes, (cx, cy, cz), cap)
    rows, groups, packs = cy // 2, cx // 4, cx // (cz // 4)
    f32, bf16 = jnp.float32, jnp.bfloat16
    dma = pltpu.SemaphoreType.DMA
    whole = pl.BlockSpec(memory_space=pltpu.VMEM)
    anywhere = pl.BlockSpec(memory_space=pl.ANY)
    return pl.pallas_call(
        functools.partial(kernel, sizes),
        out_shape=(
            jax.ShapeDtypeStruct(velocity.shape, f32),
            jax.ShapeDtypeStruct(point_force.shape, f32),
        ),
        in_specs=[anywhere] * 2 + [whole] * 4,
        out_specs=(anywhere, whole),
        scratch_shapes=[
            pltpu.VMEM((3, 3, cx + 4, cy + 16, cz), f32),
            pltpu.VMEM((cx, cy, cz), f32),
            pltpu.VMEM((3, cx, cy, cz), f32),
            dma((4,)),
            pltpu.VMEM((2, rows * cz, 3 * cx), f32),
            pltpu.VMEM((2, 3 * cx * rows, cz), f32),
            pltpu.VMEM((rows * cz, 2 * cap), bf16),
            pltpu.VMEM((rows * cz, 2 * cap), bf16),
            pltpu.VMEM((3, cx * rows, 2 * cap), f32),
            pltpu.VMEM((2, 3 * cx * rows, 2 * cz), bf16),
            pltpu.VMEM((run_count, 8, cap), f32),
            pltpu.VMEM((run_count, cap), jnp.int32),
            pltpu.VMEM((27, 8, cap), f32),
            pltpu.VMEM((28, 8, cap), f32),
            pltpu.VMEM((28, 8, cap), f32),
            pltpu.VMEM((27, 8, cap), f32),
            pltpu.VMEM((3, 2, 3, groups, 8, cz), f32),
            pltpu.VMEM((3, 2, 3, groups, 8, cz), f32),
            pltpu.VMEM((3, 2, 3, packs, rows, cz), f32),
            pltpu.VMEM((3, 2, 2, 3, packs, rows, cz), f32),
            pltpu.VMEM((3, packs, rows, cz), f32),
            dma((27,)),
            dma((27,)),
            dma((27,)),
            dma((27,)),
            dma((3, 2, 2)),
            dma((3, 2, 2)),
            dma((3, 2)),
            dma((3, 2)),
            dma((3, 2, 2)),
            dma((3, 2, 2)),
        ],
        compiler_params=pltpu.CompilerParams(
            collective_id=0, has_side_effects=True, vmem_limit_bytes=56 * 2**20
        ),
        name="farm_step",
    )(
        velocity,
        viscosity,
        point_force,
        point_offset,
        point_cell.reshape(run_count, cap),
        point_tile.reshape(run_count, cap),
    )


def solution(mesh):
    in_specs = (
        P(None, "gx", "gy", "gz"),
        P("gx", "gy", "gz"),
        P(None, ("gx", "gy", "gz")),
        P(None, ("gx", "gy", "gz")),
        P(("gx", "gy", "gz")),
        P(("gx", "gy", "gz"), None),
    )
    out_specs = (P(None, "gx", "gy", "gz"), P(None, ("gx", "gy", "gz")))
    return jax.shard_map(
        per_device, mesh=mesh, in_specs=in_specs, out_specs=out_specs, check_vma=False
    )
```

```python
import functools
import math

import jax
import jax.numpy as jnp
from jax import lax
from jax.experimental import pallas as pl
from jax.experimental.pallas import tpu as pltpu
from jax.sharding import PartitionSpec as P

MESH = pl.DeviceIdType.MESH
time_step = 0.1
kernel_width = 2.0
one_third = 1.0 / 3.0
two_thirds = 2.0 / 3.0
run_count = 8
step_blocks = 6


def split_by(x, n):
    if n & (n - 1) == 0:
        bits = n.bit_length() - 1
        return lax.shift_right_logical(x, jnp.int32(bits)), x & (n - 1)
    return lax.div(x, jnp.int32(n)), lax.rem(x, jnp.int32(n))


def halves(x):
    high = x.astype(jnp.bfloat16)
    low = (x - high.astype(jnp.float32)).astype(jnp.bfloat16)
    return high, low


def weights(centre, cells):
    middles = lax.broadcasted_iota(jnp.int32, (cells, centre.shape[1]), 0).astype(jnp.float32) + 0.5
    scaled = (middles - centre) / kernel_width
    unscaled = jnp.exp(-scaled * scaled)
    return unscaled * (1.0 / jnp.sum(unscaled, axis=0, keepdims=True))


def kernel(
    sizes,
    vel,
    visc_in,
    force,
    offset,
    cell,
    tile,
    out_vel,
    out_pts,
    field,
    visc,
    fresh,
    local_sem,
    wx_kept,
    wy_kept,
    right_kept,
    force_acc,
    forcing,
    w_high,
    w_low,
    product,
    v_split,
    vals,
    neighbour,
    pay,
    slots,
    sampled,
    returned,
    y_send,
    y_recv,
    z_send,
    z_recv,
    z_mix,
    pay_ss,
    pay_rs,
    ret_ss,
    ret_rs,
    x_ss,
    x_rs,
    y_ss,
    y_rs,
    z_ss,
    z_rs,
):
    (na, nb, nc), (cx, cy, cz), cap = sizes
    a, b, c = (lax.axis_index(axis) for axis in ("gx", "gy", "gz"))
    where_am_i = (a, b, c)
    counts = (na, nb, nc)
    half_planes = cx // 2
    groups = half_planes // 4

    def step_of(n):
        return n // 9 - 1, n // 3 % 3 - 1, n % 3 - 1

    def inside(place):
        ok = (place[0] >= 0) & (place[0] < na)
        ok &= (place[1] >= 0) & (place[1] < nb)
        return ok & (place[2] >= 0) & (place[2] < nc)

    def target_of(n, sign):
        da, db, dc = step_of(n)
        return a + sign * da, b + sign * db, c + sign * dc

    vel_copy = pltpu.make_async_copy(
        vel, field.at[0, :, pl.ds(2, cx), pl.ds(8, cy)], local_sem.at[0]
    )
    vel_copy.start()
    visc_copy = pltpu.make_async_copy(visc_in, visc, local_sem.at[1])
    visc_copy.start()

    slots[...] = jnp.zeros_like(slots)
    returned[...] = jnp.zeros_like(returned)
    y_recv[...] = jnp.zeros_like(y_recv)
    z_recv[...] = jnp.zeros_like(z_recv)
    edge = jnp.zeros((3, 2) + field.shape[3:], jnp.float32)
    for s in range(3):
        field[s, :, 0:2] = edge
        field[s, :, cx + 2 : cx + 4] = edge

    barrier = pltpu.get_barrier_semaphore()

    def greet(n, carry):
        place = target_of(n, 1)

        @pl.when(inside(place) & (n != 13))
        def _():
            pl.semaphore_signal(barrier, inc=1, device_id=place, device_id_type=MESH)

        return carry

    lax.fori_loop(0, 27, greet, 0)

    codes = cell[...]
    code_a, rest = split_by(codes, cy * cz)
    code_b, code_c = split_by(rest, cz)
    tiles = tile[...]
    tile_a, rest = split_by(tiles, nb * nc)
    tile_b, tile_c = split_by(rest, nc)
    neighbour[...] = ((tile_a - a + 1) * 3 + tile_b - b + 1) * 3 + tile_c - c + 1
    vals[...] = jnp.zeros_like(vals)
    for r in range(run_count):
        span = slice(r * cap, (r + 1) * cap)
        vals[r, 0:3, :] = force[:, span]
        for d, code in enumerate((code_a, code_b, code_c)):
            vals[r, 3 + d : 4 + d, :] = code[r : r + 1].astype(jnp.float32) + offset[d : d + 1, span]

    pl.semaphore_wait(
        barrier,
        (1 + (a > 0).astype(jnp.int32) + (a < na - 1).astype(jnp.int32))
        * (1 + (b > 0).astype(jnp.int32) + (b < nb - 1).astype(jnp.int32))
        * (1 + (c > 0).astype(jnp.int32) + (c < nc - 1).astype(jnp.int32))
        - 1,
    )

    def pay_copy(n, place):
        return pltpu.make_async_remote_copy(
            pay.at[n], slots.at[n], pay_ss.at[n], pay_rs.at[n], device_id=place, device_id_type=MESH
        )

    def send_points(n, carry):
        block = jnp.zeros(vals.shape[1:], jnp.float32)
        for r in range(run_count):
            block = jnp.where(neighbour[r : r + 1, :] == n, vals[r], block)
        pay[n] = block
        place = target_of(n, 1)

        @pl.when(inside(place) & (n != 13))
        def _():
            pay_copy(n, place).start()

        return carry

    lax.fori_loop(0, 27, send_points, 0)
    slots[13] = pay[13]

    lane = lax.broadcasted_iota(jnp.int32, (cy, cz), 1)

    def pack_plane(s, h, g, t, v):
        within = 4 * g + t
        for comp in range(3):
            y_send[s, 0, h, comp, g, 2 * t : 2 * t + 2, :] = v[comp][0:2]
            y_send[s, 1, h, comp, g, 2 * t : 2 * t + 2, :] = v[comp][cy - 2 : cy]
            moved = pltpu.roll(v[comp], 4 * within + 2, 1)
            z_send[s, h, comp] = jnp.where((lane >> 2) == within, moved, z_send[s, h, comp])

    def beside(dim, side):
        step = 2 * side - 1
        place = tuple(p + step if d == dim else p for d, p in enumerate(where_am_i))
        ok = place[dim] >= 0 if side == 0 else place[dim] < counts[dim]
        return place, ok

    def x_copy(s, side, place):
        source, target = (2, cx + 2) if side == 0 else (cx, 0)
        rows = slice(8, 8 + cy)
        return pltpu.make_async_remote_copy(
            field.at[s, :, pl.ds(source, 2), rows],
            field.at[s, :, pl.ds(target, 2), rows],
            x_ss.at[s, side],
            x_rs.at[s, side],
            device_id=place,
            device_id_type=MESH,
        )

    def y_copy(s, side, h, place):
        return pltpu.make_async_remote_copy(
            y_send.at[s, side, h],
            y_recv.at[s, side, h],
            y_ss.at[s, side, h],
            y_rs.at[s, side, h],
            device_id=place,
            device_id_type=MESH,
        )

    def z_copy(s, side, h, place):
        return pltpu.make_async_remote_copy(
            z_send.at[s, h],
            z_recv.at[s, side, h],
            z_ss.at[s, side, h],
            z_rs.at[s, side, h],
            device_id=place,
            device_id_type=MESH,
        )

    def send_half(s, h):
        for side in (0, 1):
            place, ok = beside(1, side)
            pl.when(ok)(lambda: y_copy(s, side, h, place).start())
        for side in (0, 1):
            place, ok = beside(2, side)
            pl.when(ok)(lambda: z_copy(s, side, h, place).start())
            place, ok = beside(0, side)
            pl.when(ok & (h == side))(lambda: x_copy(s, side, place).start())

    def wait_half(s, h):
        for side in (0, 1):
            place, ok = beside(0, 1 - side)
            pl.when(ok & (h == 1 - side))(lambda: x_copy(s, side, place).wait_recv())
            place, ok = beside(2, 1 - side)
            pl.when(ok)(lambda: z_copy(s, side, h, place).wait_recv())
            place, ok = beside(1, 1 - side)
            pl.when(ok)(lambda: y_copy(s, side, h, place).wait_recv())

    def wait_sends(s):
        for side in (0, 1):
            place, ok = beside(0, side)
            pl.when(ok)(lambda: x_copy(s, side, place).wait_send())
            for h in (0, 1):
                place, ok = beside(1, side)
                pl.when(ok)(lambda: y_copy(s, side, h, place).wait_send())
                place, ok = beside(2, side)
                pl.when(ok)(lambda: z_copy(s, side, h, place).wait_send())

    first = lax.rem(a, 2)
    z_send[...] = jnp.zeros_like(z_send)
    vel_copy.wait()

    for turn in range(2):
        h = first if turn == 0 else 1 - first

        def stage_in(g, carry):
            for t in range(4):
                i = h * half_planes + 4 * g + t
                v = [field[0, comp, i + 2, 8 : 8 + cy, :] for comp in range(3)]
                pack_plane(0, h, g, t, v)
            return carry

        lax.fori_loop(0, groups, stage_in, 0)
        send_half(0, h)

    def span_of(p, count):
        low = jnp.where(p < count - 1, 0, 1)
        high = jnp.where(p > 0, 2, 1)
        return low, high - low + 1

    (low_a, in_a), (low_b, in_b), (low_c, in_c) = (
        span_of(p, count) for p, count in zip(where_am_i, counts)
    )
    blocks = in_a * in_b * in_c
    steps = (blocks + step_blocks - 1) // step_blocks

    def block_of(v):
        n = (low_a + v // (in_b * in_c)) * 9 + (low_b + v // in_c % in_b) * 3 + low_c + v % in_c
        return jnp.where(v < blocks, n, 27)

    def wait_points(n, carry):
        place = target_of(n, -1)

        @pl.when(inside(place) & (n != 13))
        def _():
            pay_copy(n, place).wait_recv()

        return carry

    lax.fori_loop(0, 27, wait_points, 0)

    def blocks_of(step):
        return [block_of(step_blocks * step + m) for m in range(step_blocks)]

    force_acc[...] = jnp.zeros_like(force_acc)

    def spread(step, carry):
        s = jnp.concatenate([slots[n] for n in blocks_of(step)], axis=1)
        wx = weights(s[3:4], cx)
        wy = weights(s[4:5], cy)
        wz = weights(s[5:6], cz)
        wx_kept[step] = wx
        wy_kept[step] = wy
        z_high, z_low = halves(wz)
        for m, part in enumerate((z_high, z_high, z_low, z_low)):
            right_kept[step, m * cz : (m + 1) * cz, :] = part
        a_high, a_low = halves(jnp.concatenate([s[d : d + 1] * wx for d in range(3)], axis=0))
        for j in range(cy):
            high, low = halves(wy[j : j + 1] * wz)
            w_high[j * cz : (j + 1) * cz, :] = high
            w_low[j * cz : (j + 1) * cz, :] = low
        right = jnp.concatenate([a_high, a_low, a_high], axis=1)
        left = jnp.concatenate([w_high[...], w_high[...], w_low[...]], axis=1)
        force_acc[...] += lax.dot_general(
            left, right, (((1,), (1,)), ((), ())), preferred_element_type=jnp.float32
        )
        return carry

    lax.fori_loop(0, steps, spread, 0)

    for j in range(cy):
        turned = force_acc[j * cz : (j + 1) * cz, :].T
        for comp in range(3):
            forcing[pl.ds(comp * cx * cy + j, cx, stride=cy), :] = turned[comp * cx : (comp + 1) * cx]

    def out_copy(h):
        span = pl.ds(h * half_planes, half_planes)
        return pltpu.make_async_copy(fresh.at[:, span], out_vel.at[:, span], local_sem.at[2 + h])

    visc_copy.wait()

    for s in range(3):
        for turn in range(2):
            h = first if turn == 0 else 1 - first
            wait_half(s, h)
            for comp in range(3):
                z_mix[comp] = jnp.where((lane & 3) < 2, z_recv[s, 1, h, comp], z_recv[s, 0, h, comp])

            def advance(g, carry):
                for t in range(4):
                    i = h * half_planes + 4 * g + t
                    centre = [field[s, comp, i + 2, 8 : 8 + cy, :] for comp in range(3)]
                    nu = visc[i]
                    result = []
                    for comp in range(3):
                        v = centre[comp]
                        field[s, comp, i + 2, 6:8, :] = y_recv[s, 1, h, comp, g, 2 * t : 2 * t + 2, :]
                        field[s, comp, i + 2, 8 + cy : 10 + cy, :] = y_recv[
                            s, 0, h, comp, g, 2 * t : 2 * t + 2, :
                        ]
                        ends = pltpu.roll(z_mix[comp], cz - 2 - 4 * (4 * g + t), 1)
                        around = (
                            [field[s, comp, i + 2 + m, 8 : 8 + cy, :] for m in (-2, -1, 1, 2)],
                            [field[s, comp, i + 2, 8 + m : 8 + m + cy, :] for m in (-2, -1, 1, 2)],
                            [
                                pltpu.roll(jnp.where(lane >= cz - 2, ends, v), 2, 1),
                                pltpu.roll(jnp.where(lane >= cz - 1, ends, v), 1, 1),
                                pltpu.roll(jnp.where(lane < 1, ends, v), cz - 1, 1),
                                pltpu.roll(jnp.where(lane < 2, ends, v), cz - 2, 1),
                            ],
                        )
                        spreading = -6.0 * v
                        carried = jnp.zeros_like(v)
                        for d in range(3):
                            m2, m1, p1, p2 = around[d]
                            carried += centre[d] * (8.0 * (p1 - m1) - (p2 - m2))
                            spreading += p1 + m1
                        row = pl.multiple_of((comp * cx + i) * cy, cy)
                        tend = nu * spreading - carried * (1.0 / 12.0) + forcing[pl.ds(row, cy), :]
                        moved = v + time_step * tend
                        if s == 1:
                            moved = 0.75 * field[0, comp, i + 2, 8 : 8 + cy, :] + 0.25 * moved
                        elif s == 2:
                            moved = one_third * field[0, comp, i + 2, 8 : 8 + cy, :] + two_thirds * moved
                        result.append(moved)
                        if s < 2:
                            field[s + 1, comp, i + 2, 8 : 8 + cy, :] = moved
                        else:
                            fresh[comp, i] = moved
                            high, low = halves(moved)
                            v_split[pl.ds(row, cy), 0:cz] = high
                            v_split[pl.ds(row, cy), cz : 2 * cz] = low
                    if s < 2:
                        pack_plane(s + 1, h, g, t, result)
                return carry

            lax.fori_loop(0, groups, advance, 0)
            if s < 2:
                send_half(s + 1, h)
            else:
                out_copy(h).start()

    def ret_copy(n, place):
        return pltpu.make_async_remote_copy(
            sampled.at[n],
            returned.at[n],
            ret_ss.at[n],
            ret_rs.at[n],
            device_id=place,
            device_id_type=MESH,
        )

    sampled[...] = jnp.zeros_like(sampled)

    def sample(step, carry):
        places = blocks_of(step)
        right = right_kept[step]
        for comp in range(3):
            v = v_split[comp * cx * cy : (comp + 1) * cx * cy, :]
            product[comp] = jnp.dot(
                jnp.concatenate([v, v], axis=1), right, preferred_element_type=jnp.float32
            )
        for comp in range(3):
            total = jnp.zeros((cy, step_blocks * cap), jnp.float32)
            for i in range(cx):
                total += wx_kept[step, i : i + 1, :] * product[comp, i * cy : (i + 1) * cy, :]
            row = jnp.sum(total * wy_kept[step], axis=0, keepdims=True)
            for m, n in enumerate(places):
                sampled[n, comp : comp + 1, :] = row[:, m * cap : (m + 1) * cap]
        for n in places:

            @pl.when((n != 13) & (n < 27))
            def _():
                ret_copy(n, target_of(n, -1)).start()

        return carry

    lax.fori_loop(0, steps, sample, 0)
    returned[13] = sampled[13]

    def wait_returned(n, carry):
        @pl.when(inside(target_of(n, 1)) & (n != 13))
        def _():
            ret_copy(n, target_of(n, 1)).wait_recv()

        return carry

    lax.fori_loop(0, 27, wait_returned, 0)
    for r in range(run_count):

        def pick(n, block):
            return jnp.where(neighbour[r : r + 1, :] == n, returned[n], block)

        block = lax.fori_loop(0, 27, pick, jnp.zeros(returned.shape[1:], jnp.float32), unroll=True)
        out_pts[:, r * cap : (r + 1) * cap] = block[0:3]

    def finish(n, carry):
        @pl.when(inside(target_of(n, 1)) & (n != 13))
        def _():
            pay_copy(n, target_of(n, 1)).wait_send()

        @pl.when(inside(target_of(n, -1)) & (n != 13))
        def _():
            ret_copy(n, target_of(n, -1)).wait_send()

        return carry

    lax.fori_loop(0, 27, finish, 0)
    for s in range(3):
        wait_sends(s)
    for h in range(2):
        out_copy(h).wait()


def per_device(velocity, viscosity, point_force, point_offset, point_cell, point_tile):
    _, cx, cy, cz = velocity.shape
    points = point_force.shape[1]
    cap = points // run_count
    mesh_sizes = tuple(lax.axis_size(axis) for axis in ("gx", "gy", "gz"))
    sizes = (mesh_sizes, (cx, cy, cz), cap)
    half, groups = cx // 2, cx // 8
    f32, bf16 = jnp.float32, jnp.bfloat16
    dma = pltpu.SemaphoreType.DMA
    whole = pl.BlockSpec(memory_space=pltpu.VMEM)
    anywhere = pl.BlockSpec(memory_space=pl.ANY)
    most = math.prod(min(3, n) for n in mesh_sizes)
    steps = -(-most // step_blocks)
    width = step_blocks * cap
    return pl.pallas_call(
        functools.partial(kernel, sizes),
        out_shape=(
            jax.ShapeDtypeStruct(velocity.shape, f32),
            jax.ShapeDtypeStruct(point_force.shape, f32),
        ),
        in_specs=[anywhere] * 2 + [whole] * 4,
        out_specs=(anywhere, whole),
        scratch_shapes=[
            pltpu.VMEM((3, 3, cx + 4, cy + 16, cz), f32),
            pltpu.VMEM((cx, cy, cz), f32),
            pltpu.VMEM((3, cx, cy, cz), f32),
            dma((4,)),
            pltpu.VMEM((steps, cx, width), f32),
            pltpu.VMEM((steps, cy, width), f32),
            pltpu.VMEM((steps, 4 * cz, width), bf16),
            pltpu.VMEM((cy * cz, 3 * cx), f32),
            pltpu.VMEM((3 * cx * cy, cz), f32),
            pltpu.VMEM((cy * cz, width), bf16),
            pltpu.VMEM((cy * cz, width), bf16),
            pltpu.VMEM((3, cx * cy, width), f32),
            pltpu.VMEM((3 * cx * cy, 2 * cz), bf16),
            pltpu.VMEM((run_count, 8, cap), f32),
            pltpu.VMEM((run_count, cap), jnp.int32),
            pltpu.VMEM((27, 8, cap), f32),
            pltpu.VMEM((28, 8, cap), f32),
            pltpu.VMEM((28, 8, cap), f32),
            pltpu.VMEM((27, 8, cap), f32),
            pltpu.VMEM((3, 2, 2, 3, groups, 8, cz), f32),
            pltpu.VMEM((3, 2, 2, 3, groups, 8, cz), f32),
            pltpu.VMEM((3, 2, 3, cy, cz), f32),
            pltpu.VMEM((3, 2, 2, 3, cy, cz), f32),
            pltpu.VMEM((3, cy, cz), f32),
            dma((27,)),
            dma((27,)),
            dma((27,)),
            dma((27,)),
            dma((3, 2)),
            dma((3, 2)),
            dma((3, 2, 2)),
            dma((3, 2, 2)),
            dma((3, 2, 2)),
            dma((3, 2, 2)),
        ],
        compiler_params=pltpu.CompilerParams(
            collective_id=0, has_side_effects=True, vmem_limit_bytes=56 * 2**20
        ),
        name="farm_step",
    )(
        velocity,
        viscosity,
        point_force,
        point_offset,
        point_cell.reshape(run_count, cap),
        point_tile.reshape(run_count, cap),
    )


def solution(mesh):
    in_specs = (
        P(None, "gx", "gy", "gz"),
        P("gx", "gy", "gz"),
        P(None, ("gx", "gy", "gz")),
        P(None, ("gx", "gy", "gz")),
        P(("gx", "gy", "gz")),
        P(("gx", "gy", "gz"), None),
    )
    out_specs = (P(None, "gx", "gy", "gz"), P(None, ("gx", "gy", "gz")))
    return jax.shard_map(
        per_device, mesh=mesh, in_specs=in_specs, out_specs=out_specs, check_vma=False
    )
```

```python
import functools
import math

import jax
import jax.numpy as jnp
from jax import lax
from jax.experimental import pallas as pl
from jax.experimental.pallas import tpu as pltpu
from jax.sharding import PartitionSpec as P

MESH = pl.DeviceIdType.MESH
time_step = 0.1
kernel_width = 2.0
one_third = 1.0 / 3.0
two_thirds = 2.0 / 3.0
run_count = 8
step_blocks = 6


def split_by(x, n):
    if n & (n - 1) == 0:
        bits = n.bit_length() - 1
        return lax.shift_right_logical(x, jnp.int32(bits)), x & (n - 1)
    return lax.div(x, jnp.int32(n)), lax.rem(x, jnp.int32(n))


def halves(x):
    high = x.astype(jnp.bfloat16)
    low = (x - high.astype(jnp.float32)).astype(jnp.bfloat16)
    return high, low


def weights(centre, cells):
    middles = lax.broadcasted_iota(jnp.int32, (cells, centre.shape[1]), 0).astype(jnp.float32) + 0.5
    scaled = (middles - centre) / kernel_width
    unscaled = jnp.exp(-scaled * scaled)
    return unscaled * (1.0 / jnp.sum(unscaled, axis=0, keepdims=True))


def kernel(
    sizes,
    vel,
    visc_in,
    force,
    offset,
    cell,
    tile,
    out_vel,
    out_pts,
    field,
    visc,
    fresh,
    local_sem,
    wx_kept,
    wy_kept,
    wz_kept,
    force_kept,
    right_kept,
    force_acc,
    forcing,
    w_high,
    w_low,
    product,
    v_split,
    vals,
    neighbour,
    pay,
    slots,
    sampled,
    returned,
    y_send,
    y_recv,
    z_send,
    z_recv,
    z_mix,
    pay_ss,
    pay_rs,
    ret_ss,
    ret_rs,
    x_ss,
    x_rs,
    y_ss,
    y_rs,
    z_ss,
    z_rs,
):
    (na, nb, nc), (cx, cy, cz), cap = sizes
    a, b, c = (lax.axis_index(axis) for axis in ("gx", "gy", "gz"))
    where_am_i = (a, b, c)
    counts = (na, nb, nc)
    rows = cy // 2
    pack_groups = cz // 16
    packs = cx // (cz // 4)

    def step_of(n):
        return n // 9 - 1, n // 3 % 3 - 1, n % 3 - 1

    def inside(place):
        ok = (place[0] >= 0) & (place[0] < na)
        ok &= (place[1] >= 0) & (place[1] < nb)
        return ok & (place[2] >= 0) & (place[2] < nc)

    def target_of(n, sign):
        da, db, dc = step_of(n)
        return a + sign * da, b + sign * db, c + sign * dc

    vel_copy = pltpu.make_async_copy(
        vel, field.at[0, :, pl.ds(2, cx), pl.ds(8, cy)], local_sem.at[0]
    )
    vel_copy.start()
    visc_copy = pltpu.make_async_copy(visc_in, visc, local_sem.at[1])
    visc_copy.start()

    slots[...] = jnp.zeros_like(slots)
    returned[...] = jnp.zeros_like(returned)
    y_recv[...] = jnp.zeros_like(y_recv)
    z_recv[...] = jnp.zeros_like(z_recv)
    edge = jnp.zeros((3, 2) + field.shape[3:], jnp.float32)
    for s in range(3):
        field[s, :, 0:2] = edge
        field[s, :, cx + 2 : cx + 4] = edge

    barrier = pltpu.get_barrier_semaphore()

    def greet(n, carry):
        place = target_of(n, 1)

        @pl.when(inside(place) & (n != 13))
        def _():
            pl.semaphore_signal(barrier, inc=1, device_id=place, device_id_type=MESH)

        return carry

    lax.fori_loop(0, 27, greet, 0)

    codes = cell[...]
    code_a, rest = split_by(codes, cy * cz)
    code_b, code_c = split_by(rest, cz)
    tiles = tile[...]
    tile_a, rest = split_by(tiles, nb * nc)
    tile_b, tile_c = split_by(rest, nc)
    neighbour[...] = ((tile_a - a + 1) * 3 + tile_b - b + 1) * 3 + tile_c - c + 1
    vals[...] = jnp.zeros_like(vals)
    for r in range(run_count):
        span = slice(r * cap, (r + 1) * cap)
        vals[r, 0:3, :] = force[:, span]
        for d, code in enumerate((code_a, code_b, code_c)):
            vals[r, 3 + d : 4 + d, :] = code[r : r + 1].astype(jnp.float32) + offset[d : d + 1, span]

    pl.semaphore_wait(
        barrier,
        (1 + (a > 0).astype(jnp.int32) + (a < na - 1).astype(jnp.int32))
        * (1 + (b > 0).astype(jnp.int32) + (b < nb - 1).astype(jnp.int32))
        * (1 + (c > 0).astype(jnp.int32) + (c < nc - 1).astype(jnp.int32))
        - 1,
    )

    def pay_copy(n, place):
        return pltpu.make_async_remote_copy(
            pay.at[n], slots.at[n], pay_ss.at[n], pay_rs.at[n], device_id=place, device_id_type=MESH
        )

    def send_points(n, carry):
        block = jnp.zeros(vals.shape[1:], jnp.float32)
        for r in range(run_count):
            block = jnp.where(neighbour[r : r + 1, :] == n, vals[r], block)
        pay[n] = block
        place = target_of(n, 1)

        @pl.when(inside(place) & (n != 13))
        def _():
            pay_copy(n, place).start()

        return carry

    lax.fori_loop(0, 27, send_points, 0)
    slots[13] = pay[13]

    lane = lax.broadcasted_iota(jnp.int32, (rows, cz), 1)

    def pack_planes(s, h, g, planes):
        inner = slice(0, 2) if h == 0 else slice(rows - 2, rows)
        pack, place = g // pack_groups, g % pack_groups
        for comp in range(3):
            packed = z_send[s, h, comp, pack]
            for t in range(4):
                v = planes[t][comp]
                y_send[s, h, comp, g, 2 * t : 2 * t + 2, :] = v[inner]
                within = 4 * place + t
                packed = jnp.where((lane >> 2) == within, pltpu.roll(v, 4 * within + 2, 1), packed)
            z_send[s, h, comp, pack] = packed

    def beside(dim, side):
        step = 2 * side - 1
        place = tuple(p + step if d == dim else p for d, p in enumerate(where_am_i))
        ok = place[dim] >= 0 if side == 0 else place[dim] < counts[dim]
        return place, ok

    def x_copy(s, side, h, place):
        source, target = (2, cx + 2) if side == 0 else (cx, 0)
        span = slice(8 + rows * h, 8 + rows * (h + 1))
        return pltpu.make_async_remote_copy(
            field.at[s, :, pl.ds(source, 2), span],
            field.at[s, :, pl.ds(target, 2), span],
            x_ss.at[s, side, h],
            x_rs.at[s, side, h],
            device_id=place,
            device_id_type=MESH,
        )

    def y_copy(s, side, place):
        return pltpu.make_async_remote_copy(
            y_send.at[s, side],
            y_recv.at[s, side],
            y_ss.at[s, side],
            y_rs.at[s, side],
            device_id=place,
            device_id_type=MESH,
        )

    def z_copy(s, side, h, place):
        return pltpu.make_async_remote_copy(
            z_send.at[s, h],
            z_recv.at[s, side, h],
            z_ss.at[s, side, h],
            z_rs.at[s, side, h],
            device_id=place,
            device_id_type=MESH,
        )

    def send_half(s, h):
        place, ok = beside(1, h)
        pl.when(ok)(lambda: y_copy(s, h, place).start())
        for side in (0, 1):
            z_place, z_ok = beside(2, side)
            pl.when(z_ok)(lambda: z_copy(s, side, h, z_place).start())
            x_place, x_ok = beside(0, side)
            pl.when(x_ok)(lambda: x_copy(s, side, h, x_place).start())

    def wait_half(s, h):
        for side in (0, 1):
            x_place, x_ok = beside(0, 1 - side)
            pl.when(x_ok)(lambda: x_copy(s, side, h, x_place).wait_recv())
            z_place, z_ok = beside(2, 1 - side)
            pl.when(z_ok)(lambda: z_copy(s, side, h, z_place).wait_recv())
        place, ok = beside(1, h)
        pl.when(ok)(lambda: y_copy(s, 1 - h, place).wait_recv())

    def wait_sends(s):
        for side in (0, 1):
            y_place, y_ok = beside(1, side)
            pl.when(y_ok)(lambda: y_copy(s, side, y_place).wait_send())
            x_place, x_ok = beside(0, side)
            z_place, z_ok = beside(2, side)
            for h in (0, 1):
                pl.when(x_ok)(lambda: x_copy(s, side, h, x_place).wait_send())
                pl.when(z_ok)(lambda: z_copy(s, side, h, z_place).wait_send())

    first = lax.rem(b, 2)

    def by_turn(turn, work):
        pl.when(first == turn)(lambda: work(0))
        pl.when(first != turn)(lambda: work(1))

    def half_of(turn):
        return first if turn == 0 else 1 - first

    z_send[...] = jnp.zeros_like(z_send)
    vel_copy.wait()

    def first_faces(h):
        def one(g, carry):
            span = slice(8 + rows * h, 8 + rows * (h + 1))
            pack_planes(
                0, h, g, [[field[0, comp, 4 * g + t + 2, span, :] for comp in range(3)] for t in range(4)]
            )
            return carry

        lax.fori_loop(0, cx // 4, one, 0)
        send_half(0, h)

    for turn in range(2):
        by_turn(turn, first_faces)

    def span_of(p, count):
        low = jnp.where(p < count - 1, 0, 1)
        high = jnp.where(p > 0, 2, 1)
        return low, high - low + 1

    (low_a, in_a), (low_b, in_b), (low_c, in_c) = (
        span_of(p, count) for p, count in zip(where_am_i, counts)
    )
    blocks = in_a * in_b * in_c
    steps = (blocks + step_blocks - 1) // step_blocks

    def block_of(v):
        n = (low_a + v // (in_b * in_c)) * 9 + (low_b + v // in_c % in_b) * 3 + low_c + v % in_c
        return jnp.where(v < blocks, n, 27)

    def wait_points(n, carry):
        place = target_of(n, -1)

        @pl.when(inside(place) & (n != 13))
        def _():
            pay_copy(n, place).wait_recv()

        return carry

    lax.fori_loop(0, 27, wait_points, 0)

    def blocks_of(step):
        return [block_of(step_blocks * step + m) for m in range(step_blocks)]

    def prepare(step, carry):
        s = jnp.concatenate([slots[n] for n in blocks_of(step)], axis=1)
        wx = weights(s[3:4], cx)
        wz = weights(s[5:6], cz)
        wx_kept[step] = wx
        wy_kept[step] = weights(s[4:5], cy)
        wz_kept[step] = wz
        z_high, z_low = halves(wz)
        for m, part in enumerate((z_high, z_high, z_low, z_low)):
            right_kept[step, m * cz : (m + 1) * cz, :] = part
        for d in range(3):
            a_high, a_low = halves(s[d : d + 1] * wx)
            for m, part in enumerate((a_high, a_low, a_high)):
                force_kept[step, d * cx : (d + 1) * cx, m * width : (m + 1) * width] = part
        return carry

    width = step_blocks * cap
    lax.fori_loop(0, steps, prepare, 0)
    force_acc[...] = jnp.zeros_like(force_acc)
    visc_copy.wait()

    def half_rows(w, h):
        return jnp.where(h == 0, w[:rows], w[rows:])

    def spread_half(turn):
        h = half_of(turn)

        def spread(step, carry):
            wy = half_rows(wy_kept[step], h)
            wz = wz_kept[step]
            for j in range(rows):
                high, low = halves(wy[j : j + 1] * wz)
                w_high[j * cz : (j + 1) * cz, :] = high
                w_low[j * cz : (j + 1) * cz, :] = low
            right = force_kept[step]
            left = jnp.concatenate([w_high[...], w_high[...], w_low[...]], axis=1)
            force_acc[turn] += lax.dot_general(
                left, right, (((1,), (1,)), ((), ())), preferred_element_type=jnp.float32
            )
            return carry

        lax.fori_loop(0, steps, spread, 0)
        for j in range(rows):
            turned = force_acc[turn, j * cz : (j + 1) * cz, :].T
            for comp in range(3):
                forcing[turn, pl.ds(comp * cx * rows + j, cx, stride=rows), :] = turned[
                    comp * cx : (comp + 1) * cx
                ]

    def advance_half(s, turn, h):
        wait_half(s, h)
        for comp in range(3):
            for pack in range(packs):
                z_mix[comp, pack] = jnp.where(
                    (lane & 3) < 2, z_recv[s, 1, h, comp, pack], z_recv[s, 0, h, comp, pack]
                )
        low = 8 + rows * h
        span = slice(low, low + rows)
        halo = slice(6, 8) if h == 0 else slice(8 + cy, 10 + cy)

        def advance(g, carry):
            pack, place = g // pack_groups, g % pack_groups
            planes = []
            for t in range(4):
                i = 4 * g + t
                centre = [field[s, comp, i + 2, span, :] for comp in range(3)]
                nu = visc[i, rows * h : rows * (h + 1), :]
                result = []
                for comp in range(3):
                    v = centre[comp]
                    field[s, comp, i + 2, halo, :] = y_recv[s, 1 - h, comp, g, 2 * t : 2 * t + 2, :]
                    ends = pltpu.roll(z_mix[comp, pack], cz - 2 - 4 * (4 * place + t), 1)
                    around = (
                        [field[s, comp, i + 2 + m, span, :] for m in (-2, -1, 1, 2)],
                        [field[s, comp, i + 2, low + m : low + m + rows, :] for m in (-2, -1, 1, 2)],
                        [
                            pltpu.roll(jnp.where(lane >= cz - 2, ends, v), 2, 1),
                            pltpu.roll(jnp.where(lane >= cz - 1, ends, v), 1, 1),
                            pltpu.roll(jnp.where(lane < 1, ends, v), cz - 1, 1),
                            pltpu.roll(jnp.where(lane < 2, ends, v), cz - 2, 1),
                        ],
                    )
                    spreading = -6.0 * v
                    carried = jnp.zeros_like(v)
                    for d in range(3):
                        m2, m1, p1, p2 = around[d]
                        carried += centre[d] * (8.0 * (p1 - m1) - (p2 - m2))
                        spreading += p1 + m1
                    row = pl.multiple_of((comp * cx + i) * rows, rows)
                    tend = nu * spreading - carried * (1.0 / 12.0) + forcing[turn, pl.ds(row, rows), :]
                    moved = v + time_step * tend
                    if s == 1:
                        moved = 0.75 * field[0, comp, i + 2, span, :] + 0.25 * moved
                    elif s == 2:
                        moved = one_third * field[0, comp, i + 2, span, :] + two_thirds * moved
                    result.append(moved)
                    if s < 2:
                        field[s + 1, comp, i + 2, span, :] = moved
                    else:
                        fresh[comp, i, rows * h : rows * (h + 1), :] = moved
                planes.append(result)
            if s < 2:
                pack_planes(s + 1, h, g, planes)
            else:
                for comp in range(3):
                    for t in (0, 2):
                        row = pl.multiple_of((comp * cx + 4 * g + t) * rows, 2 * rows)
                        high, low_part = halves(
                            jnp.concatenate([planes[t][comp], planes[t + 1][comp]], axis=0)
                        )
                        v_split[turn, pl.ds(row, 2 * rows), 0:cz] = high
                        v_split[turn, pl.ds(row, 2 * rows), cz : 2 * cz] = low_part
            return carry

        lax.fori_loop(0, cx // 4, advance, 0)
        if s < 2:
            send_half(s + 1, h)
        else:
            out_copy(h).start()

    def out_copy(h):
        span = slice(rows * h, rows * (h + 1))
        return pltpu.make_async_copy(fresh.at[:, :, span], out_vel.at[:, :, span], local_sem.at[2 + h])

    def section(s, turn):
        by_turn(turn, lambda h: advance_half(s, turn, h))

    spread_half(0)
    section(0, 0)
    spread_half(1)
    section(0, 1)
    section(1, 0)
    section(1, 1)
    section(2, 0)

    def ret_copy(n, place):
        return pltpu.make_async_remote_copy(
            sampled.at[n],
            returned.at[n],
            ret_ss.at[n],
            ret_rs.at[n],
            device_id=place,
            device_id_type=MESH,
        )

    sampled[...] = jnp.zeros_like(sampled)

    def sample_half(turn):
        h = half_of(turn)

        def sample(step, carry):
            places = blocks_of(step)
            v = v_split[turn]
            product[...] = jnp.dot(
                jnp.concatenate([v, v], axis=1), right_kept[step], preferred_element_type=jnp.float32
            )
            wy = half_rows(wy_kept[step], h)
            for comp in range(3):
                total = jnp.zeros((rows, width), jnp.float32)
                for i in range(cx):
                    start = (comp * cx + i) * rows
                    total += wx_kept[step, i : i + 1, :] * product[start : start + rows, :]
                row = jnp.sum(total * wy, axis=0, keepdims=True)
                for m, n in enumerate(places):
                    part = row[:, m * cap : (m + 1) * cap]
                    if turn == 1:
                        part = part + sampled[n, comp : comp + 1, :]
                    sampled[n, comp : comp + 1, :] = part
            if turn == 1:
                for n in places:

                    @pl.when((n != 13) & (n < 27))
                    def _():
                        ret_copy(n, target_of(n, -1)).start()

            return carry

        lax.fori_loop(0, steps, sample, 0)

    sample_half(0)
    section(2, 1)
    sample_half(1)
    returned[13] = sampled[13]

    def wait_returned(n, carry):
        @pl.when(inside(target_of(n, 1)) & (n != 13))
        def _():
            ret_copy(n, target_of(n, 1)).wait_recv()

        return carry

    lax.fori_loop(0, 27, wait_returned, 0)
    for r in range(run_count):

        def pick(n, block):
            return jnp.where(neighbour[r : r + 1, :] == n, returned[n], block)

        block = lax.fori_loop(0, 27, pick, jnp.zeros(returned.shape[1:], jnp.float32), unroll=True)
        out_pts[:, r * cap : (r + 1) * cap] = block[0:3]

    def finish(n, carry):
        @pl.when(inside(target_of(n, 1)) & (n != 13))
        def _():
            pay_copy(n, target_of(n, 1)).wait_send()

        @pl.when(inside(target_of(n, -1)) & (n != 13))
        def _():
            ret_copy(n, target_of(n, -1)).wait_send()

        return carry

    lax.fori_loop(0, 27, finish, 0)
    for s in range(3):
        wait_sends(s)
    for h in range(2):
        out_copy(h).wait()


def per_device(velocity, viscosity, point_force, point_offset, point_cell, point_tile):
    _, cx, cy, cz = velocity.shape
    points = point_force.shape[1]
    cap = points // run_count
    mesh_sizes = tuple(lax.axis_size(axis) for axis in ("gx", "gy", "gz"))
    sizes = (mesh_sizes, (cx, cy, cz), cap)
    rows, groups, packs = cy // 2, cx // 4, cx // (cz // 4)
    f32, bf16 = jnp.float32, jnp.bfloat16
    dma = pltpu.SemaphoreType.DMA
    whole = pl.BlockSpec(memory_space=pltpu.VMEM)
    anywhere = pl.BlockSpec(memory_space=pl.ANY)
    most = math.prod(min(3, n) for n in mesh_sizes)
    steps = -(-most // step_blocks)
    width = step_blocks * cap
    return pl.pallas_call(
        functools.partial(kernel, sizes),
        out_shape=(
            jax.ShapeDtypeStruct(velocity.shape, f32),
            jax.ShapeDtypeStruct(point_force.shape, f32),
        ),
        in_specs=[anywhere] * 2 + [whole] * 4,
        out_specs=(anywhere, whole),
        scratch_shapes=[
            pltpu.VMEM((3, 3, cx + 4, cy + 16, cz), f32),
            pltpu.VMEM((cx, cy, cz), f32),
            pltpu.VMEM((3, cx, cy, cz), f32),
            dma((4,)),
            pltpu.VMEM((steps, cx, width), f32),
            pltpu.VMEM((steps, cy, width), f32),
            pltpu.VMEM((steps, cz, width), f32),
            pltpu.VMEM((steps, 3 * cx, 3 * width), bf16),
            pltpu.VMEM((steps, 4 * cz, width), bf16),
            pltpu.VMEM((2, rows * cz, 3 * cx), f32),
            pltpu.VMEM((2, 3 * cx * rows, cz), f32),
            pltpu.VMEM((rows * cz, width), bf16),
            pltpu.VMEM((rows * cz, width), bf16),
            pltpu.VMEM((3 * cx * rows, width), f32),
            pltpu.VMEM((2, 3 * cx * rows, 2 * cz), bf16),
            pltpu.VMEM((run_count, 8, cap), f32),
            pltpu.VMEM((run_count, cap), jnp.int32),
            pltpu.VMEM((27, 8, cap), f32),
            pltpu.VMEM((28, 8, cap), f32),
            pltpu.VMEM((28, 8, cap), f32),
            pltpu.VMEM((27, 8, cap), f32),
            pltpu.VMEM((3, 2, 3, groups, 8, cz), f32),
            pltpu.VMEM((3, 2, 3, groups, 8, cz), f32),
            pltpu.VMEM((3, 2, 3, packs, rows, cz), f32),
            pltpu.VMEM((3, 2, 2, 3, packs, rows, cz), f32),
            pltpu.VMEM((3, packs, rows, cz), f32),
            dma((27,)),
            dma((27,)),
            dma((27,)),
            dma((27,)),
            dma((3, 2, 2)),
            dma((3, 2, 2)),
            dma((3, 2)),
            dma((3, 2)),
            dma((3, 2, 2)),
            dma((3, 2, 2)),
        ],
        compiler_params=pltpu.CompilerParams(
            collective_id=0, has_side_effects=True, vmem_limit_bytes=56 * 2**20
        ),
        name="farm_step",
    )(
        velocity,
        viscosity,
        point_force,
        point_offset,
        point_cell.reshape(run_count, cap),
        point_tile.reshape(run_count, cap),
    )


def solution(mesh):
    in_specs = (
        P(None, "gx", "gy", "gz"),
        P("gx", "gy", "gz"),
        P(None, ("gx", "gy", "gz")),
        P(None, ("gx", "gy", "gz")),
        P(("gx", "gy", "gz")),
        P(("gx", "gy", "gz"), None),
    )
    out_specs = (P(None, "gx", "gy", "gz"), P(None, ("gx", "gy", "gz")))
    return jax.shard_map(
        per_device, mesh=mesh, in_specs=in_specs, out_specs=out_specs, check_vma=False
    )
```
